32 devices in a mesh: ctx: 8 (over y, x, core), head: 4 (over z).
Axes of the slice: x: 2, y: 2, z: 4, core: 2. Of those that a mesh axis runs over, the one named last changes fastest.
Arguments:
- xs: bfloat16 [4096, 5120], P('ctx', 'head'), may hold values from -6 to 6
- bmat: bfloat16 [4096, 128], P('ctx'), may hold values from -0.5 to 0.5
- cmat: bfloat16 [4096, 128], P('ctx'), may hold values from -6 to 6
- logdecay: float32 [80, 4096], P('head', 'ctx'), may hold values from -1 to 0, as said below
- starts: int32 [4096], P('ctx'), may hold values 0 or 1
- output_cotangent: bfloat16 [4096, 5120], P('ctx', 'head'), may hold values from -6 to 6
Outputs:
- input_gradient: bfloat16 [4096, 5120], P('ctx', 'head')
- grad_b: float32 [4096, 128], P(('ctx', 'head'))
- grad_c: float32 [4096, 128], P(('ctx', 'head'))
The draws below stay inside these ranges and needn't reach their ends.
Inputs may be any that keep to these rules, and one draw needn't show every extreme that they name: `logdecay`: every entry is negative.
All inputs are finite; a program needn't handle non-finite values. No bound on the sum of `starts` on one device may be relied on, other than what follows from the above.
Results may differ from the reference program's by a relative error of at most 0.001.
Values sent between devices are 32-bit elements; how exact they have to be, the bound alone decides.
A program may use at most 256 MiB of HBM per device.

```python
import math
import jax
import jax.numpy as jnp
from jax import lax

H = 80
P_SIZE = 64
N = 128
Q = 256
TOK_DEV = 512
TOKENS = 4096


def draw_logdecay(key, part):
    key = jax.random.fold_in(key, 7)
    keys = jax.random.split(key, 7)
    share = 0.5
    rough = jnp.exp(jax.random.uniform(keys[2], (H, TOKENS), jnp.float32, -0.7, 0.7))
    fast = jax.random.uniform(keys[0], (H,), jnp.float32) < share
    quick = jnp.exp(jax.random.uniform(keys[1], (H,), jnp.float32, math.log(1.0 / 50.0), math.log(1.0 / 30.0)))
    slow = jnp.exp(jax.random.uniform(keys[3], (H,), jnp.float32, math.log(0.15), math.log(0.6))) / TOKENS
    rate = jnp.where(fast, quick, slow)
    blocks = TOKENS // TOK_DEV
    block_scale = jnp.exp(jax.random.uniform(keys[4], (H, blocks, 1), jnp.float32, -0.5, 0.5))
    initial_displacement = (rate[:, None, None] * block_scale * rough.reshape(H, blocks, TOK_DEV)).reshape(H, TOKENS)
    spots = jax.random.randint(keys[5], (2,), 0, TOKENS)
    article_boundary_marks = jnp.log(jax.random.uniform(keys[6], (2,), jnp.float32, 0.55, 0.8))
    boundary_indices = jnp.arange(TOKENS)[None, :] == spots[:, None]
    packed_word_extent = jnp.sum(jnp.where(boundary_indices, article_boundary_marks[:, None], 0.0), axis=0)
    return -initial_displacement + packed_word_extent[None, :]


def plant(entries, stream_key, least, high):
    spot = [jax.random.randint(jax.random.fold_in(stream_key, axis), (), 0, length) for axis, length in enumerate(entries.shape)]
    main_axis = entries.shape.index(max(entries.shape))
    next_to = spot[:main_axis] + [(spot[main_axis] + 1) % entries.shape[main_axis]] + spot[main_axis + 1:]
    return entries.at[tuple(spot)].set(least).at[tuple(next_to)].set(high)


def steps_of(own_key, shape, pieces, smallest, largest):
    level = 1.0
    for dim, parts in pieces:
        steps = jax.random.uniform(jax.random.fold_in(jax.random.fold_in(own_key, 6), dim), (parts,), jnp.float32, smallest / len(pieces), largest / len(pieces))
        level = level * jnp.repeat(jnp.exp(steps), shape[dim] // parts).reshape((-1,) + (1,) * (len(shape) - 1 - dim))
    return level


def bell_draw(key, dims, spread, most, cuts=(), dtype=jnp.bfloat16):
    loudness = steps_of(key, dims, cuts, -0.22, 0.18) if cuts else 1.0
    array = jax.random.normal(key, dims, jnp.float32) * spread * loudness
    return jnp.minimum(jnp.maximum(array, -most), most).astype(dtype)


def setup_inputs(seed: int = 0) -> dict:
    arg_keys = jax.random.split(jax.random.key(seed), 7)
    xs = bell_draw(arg_keys[0], (TOKENS, H * P_SIZE), 1.0, 6.0, ((0, 8), (1, 4)))
    bmat = bell_draw(arg_keys[1], (TOKENS, N), N ** -0.5, 0.5, ((0, 8),))
    cmat = bell_draw(arg_keys[2], (TOKENS, N), 1.0, 6.0, ((0, 8),))
    logdecay = draw_logdecay(jax.random.fold_in(arg_keys[6], 71), 0)
    starts = plant((jax.random.randint(arg_keys[4], (TOKENS,), 0, 8 * TOK_DEV) < 1).astype(jnp.int32), jax.random.fold_in(arg_keys[4], 1), 0, 1)
    output_cotangent = bell_draw(arg_keys[5], (TOKENS, H * P_SIZE), 1.0, 6.0, ((0, 8), (1, 4)))
    return {"xs": xs, "bmat": bmat, "cmat": cmat, "logdecay": logdecay, "starts": starts, "output_cotangent": output_cotangent}


HIGH = lax.Precision.HIGHEST

def edges(decay_rows, flag_row):
    running = jnp.cumsum(decay_rows, axis=1)
    segment = jnp.cumsum(flag_row)
    enter = jnp.where(segment[None, :] == 0, jnp.exp(running), 0.0)
    tail = jnp.where(segment[None, :] == segment[-1], jnp.exp(running[:, -1:] - running), 0.0)
    passing = jnp.where(segment[-1] == 0, jnp.exp(running[:, -1]), 0.0)
    return (running, segment, enter, tail, passing)

def within_of(running, segment):
    width = segment.shape[0]
    order = jnp.arange(width)
    keep = (order[:, None] >= order[None, :]) & (segment[:, None] == segment[None, :])
    gap = running[:, :, None] - running[:, None, :]
    return jnp.where(keep[None], jnp.exp(jnp.minimum(gap, 0.0)), 0.0)

def reference(xs, bmat, cmat, logdecay, starts, output_cotangent):
    count = xs.shape[0] // Q
    heads = logdecay.shape[0]
    inputs = xs.reshape(count, Q, heads, P_SIZE)
    incoming_sensitivity = output_cotangent.reshape(count, Q, heads, P_SIZE)
    decays = logdecay.reshape(heads, count, Q).transpose(1, 0, 2)
    flags = starts.reshape(count, Q)
    keys = bmat.astype(jnp.float32).reshape(count, Q, N)
    reads = cmat.astype(jnp.float32).reshape(count, Q, N)

    def step_body(state, item):
        block, key, read, decay, flag, ups = item
        running, segment, enter, tail, passing = edges(decay, flag)
        gain = jnp.sqrt(-jnp.expm1(2.0 * decay))
        scaled = block.astype(jnp.float32) * gain.T[:, :, None]
        scores = jnp.dot(read, key.T, precision=HIGH)
        weighted = within_of(running, segment) * scores[None]
        inner = jnp.einsum('hts,shp->thp', weighted, scaled, precision=HIGH)
        carried = jnp.einsum('hpn,tn->thp', state, read, precision=HIGH) * enter.T[:, :, None]
        value = jnp.sum((inner + carried) * ups.astype(jnp.float32))
        fresh = jnp.einsum('shp,sn->hpn', scaled * tail.T[:, :, None], key, precision=HIGH)
        return (passing[:, None, None] * state + fresh, value)
    step = jax.checkpoint(step_body)

    def objective(segment_arguments, block_keys, block_reads):
        start = jnp.zeros((heads, P_SIZE, N), jnp.float32)
        final, values = lax.scan(step, start, (segment_arguments, block_keys, block_reads, decays, flags, incoming_sensitivity))
        return jnp.sum(values)
    input_gradient, grad_b, grad_c = jax.grad(objective, argnums=(0, 1, 2))(inputs, keys, reads)
    return (input_gradient.reshape(xs.shape), grad_b.reshape(bmat.shape), grad_c.reshape(cmat.shape))
```

```python
import functools

import jax
import jax.numpy as jnp
from jax import lax
from jax.experimental import pallas as pl
from jax.experimental.pallas import tpu as pltpu
from jax.sharding import PartitionSpec as P

P_SIZE = 64
N = 128
Q = 256
LANES = 128
LOG2E = 1.4426950408889634
MESH = pl.DeviceIdType.MESH
F32 = jnp.float32
BF16 = jnp.bfloat16


def nn(a, b):
    return lax.dot_general(a, b, (((1,), (0,)), ((), ())), preferred_element_type=F32)


def nt(a, b):
    return lax.dot_general(a, b, (((1,), (1,)), ((), ())), preferred_element_type=F32)


def split2(value):
    high = value.astype(BF16)
    return high, (value - high.astype(F32)).astype(BF16)


def split3(value):
    high, rest = value.astype(BF16), None
    rest = value - high.astype(F32)
    middle = rest.astype(BF16)
    return high, middle, (rest - middle.astype(F32)).astype(BF16)


def minus_expm1(x):
    series = jnp.ones_like(x)
    for term in range(11, 1, -1):
        series = 1.0 + series * x * (1.0 / term)
    return jnp.where(x > -0.5, -x * series, 1.0 - jnp.exp(x))


def kernel(
    ctx, hd, heads, count,
    xs, bm, cm, ld, st, dy,
    gx_out, gb_out, gc_out,
    ldp, colterm, runrow, factor, expand, passing, bias, scores, mixed,
    keys_t, reads_t, tail_x, t_hi, t_lo, e_hi, e_lo, group, local_s, local_a,
    agg, got0, chip, got, inout, other, final, part, rs_got,
    send_sem, recv_sem, rs_send, rs_recv,
):
    width = heads * P_SIZE
    tiles = width // LANES
    half = tiles // 2
    bits = ctx.bit_length() - 1
    me, row = lax.axis_index("ctx"), lax.axis_index("head")
    bit = [(me // (1 << d)) % 2 for d in range(bits)]
    mate = [me + (1 - 2 * bit[d]) * (1 << d) for d in range(bits)]
    core = bit[0]

    barrier = pltpu.get_barrier_semaphore()
    for d in range(bits):
        pl.semaphore_signal(barrier, inc=1, device_id={"ctx": mate[d]}, device_id_type=MESH)
    for step in range(1, hd):
        pl.semaphore_signal(
            barrier, inc=1, device_id={"head": (row + step) % hd}, device_id_type=MESH
        )

    def remote(src, dst, stage, k, d):
        return pltpu.make_async_remote_copy(
            src_ref=src, dst_ref=dst, send_sem=send_sem.at[stage, k],
            recv_sem=recv_sem.at[stage, k], device_id={"ctx": mate[d]}, device_id_type=MESH,
        )

    rows_i = lax.broadcasted_iota(jnp.int32, (Q, Q), 0)
    cols_i = lax.broadcasted_iota(jnp.int32, (Q, Q), 1)
    tri = jnp.where(rows_i >= cols_i, 1.0, 0.0).astype(BF16)
    eye = jnp.where(rows_i == cols_i, 1.0, 0.0).astype(BF16)
    ldp[...] = jnp.zeros_like(ldp)
    ldp[0:heads, :] = ld[...]
    er = lax.broadcasted_iota(jnp.int32, (LANES, width), 0)
    ec = lax.broadcasted_iota(jnp.int32, (LANES, width), 1)
    expand[...] = jnp.where(
        (ec >= er * P_SIZE) & (ec < er * P_SIZE + P_SIZE), 1.0, 0.0
    ).astype(BF16)
    hp = runrow.shape[1]
    for b in range(count):
        blk = slice(b * Q, (b + 1) * Q)
        flags = jnp.broadcast_to(st[0:1, blk].astype(F32), (LANES, Q)).astype(BF16)
        seg_col = nt(tri, flags)
        seg_row = nt(flags[0:16], tri)
        parts = split3(ldp[:, blk])
        run = nt(tri, parts[0]) + (nt(tri, parts[1]) + nt(tri, parts[2]))
        run_r = nt(parts[0][0:hp], tri) + (nt(parts[1][0:hp], tri) + nt(parts[2][0:hp], tri))
        decay = nt(eye, parts[0]) + nt(eye, parts[1]) + nt(eye, parts[2])
        gain2 = minus_expm1(2.0 * decay)
        gain = jnp.sqrt(gain2)
        runrow[b] = run_r * LOG2E
        colterm[b] = run * LOG2E - (0.5 * LOG2E) * jnp.log(gain2)
        last, seg_last = run[Q - 1 : Q], seg_col[Q - 1 : Q]
        tail = jnp.where(seg_col == seg_last, jnp.exp(last - run), 0.0) * gain
        enter = jnp.where(seg_col == 0.0, jnp.exp(run), 0.0)
        through = jnp.broadcast_to(jnp.where(seg_last == 0.0, jnp.exp(last), 0.0), (16, LANES))
        for i, value in enumerate(split3(tail)):
            factor[b, 0, i] = value
        for i, value in enumerate(split3(enter)):
            factor[b, 1, i] = value
        p3 = split3(through)
        passing[b] = (nn(p3[0], expand[...]) + nn(p3[1], expand[...]) + nn(p3[2], expand[...]))[0:8]
        keep = (cols_i >= rows_i) & (
            jnp.broadcast_to(seg_row[0:1], (Q, Q)) == jnp.broadcast_to(seg_col[:, 0:1], (Q, Q))
        )
        bias[b] = jnp.where(keep, 0.0, -1e30)
        keys_t[b] = nt(eye[0:N, 0:N], bm[blk, :]).astype(BF16)
        reads_t[b] = nt(eye[0:N, 0:N], cm[blk, :]).astype(BF16)
        scores[b] = nt(bm[blk, :], cm[blk, :])

    for k in range(tiles):
        col = slice(k * LANES, (k + 1) * LANES)
        ex = expand[:, col]
        for b in range(count):
            blk = slice(b * Q, (b + 1) * Q)
            tx = nn(factor[b, 0, 0], ex) + (nn(factor[b, 0, 1], ex) + nn(factor[b, 0, 2], ex))
            tail_x[blk, col] = tx
            hi, lo = split2(xs[blk, col].astype(F32) * tx)
            t_hi[blk, col] = hi
            t_lo[blk, col] = lo
            local_s[b, k] = nn(keys_t[b], hi) + nn(keys_t[b], lo)
            ent = nn(factor[b, 1, 0], ex) + (nn(factor[b, 1, 1], ex) + nn(factor[b, 1, 2], ex))
            hi, lo = split2(dy[blk, col].astype(F32) * ent)
            e_hi[blk, col] = hi
            e_lo[blk, col] = lo
            local_a[b, k] = nn(reads_t[b], hi) + nn(reads_t[b], lo)
        forward, backward, through = local_s[0, k], local_a[count - 1, k], passing[0, :, col]
        for b in range(1, count):
            forward = local_s[b, k] + passing[b, 0:1, col] * forward
            through = through * passing[b, :, col]
        for b in range(count - 2, -1, -1):
            backward = local_a[b, k] + passing[b, 0:1, col] * backward
        agg[k, 0:N] = forward
        agg[k, N : 2 * N] = backward
        agg[k, 2 * N : 2 * N + 8] = through

    pl.semaphore_wait(barrier, bits + hd - 1)
    stage0 = [
        remote(agg.at[(1 - core) * half + k], got0.at[k], 0, k, 0) for k in range(half)
    ]
    for copy in stage0:
        copy.start()

    F, B, T = slice(0, N), slice(N, 2 * N), slice(2 * N, 2 * N + 8)
    T1 = slice(2 * N, 2 * N + 1)
    copies = {}
    ahead = {}

    def merge(target, mine, theirs, upper):
        def low(s):
            return jnp.where(upper, theirs(s), mine(s))

        def high(s):
            return jnp.where(upper, mine(s), theirs(s))

        target[F] = high(F) + high(T1) * low(F)
        target[B] = low(B) + low(T1) * high(B)
        target[T] = low(T) * high(T)

    def chip_send(d, k):
        if d == bits - 1:
            copy = remote(
                chip.at[d - 1, k, pl.ds(pl.multiple_of(bit[d] * N, N), N)],
                got.at[d - 1, k, pl.ds(0, N)], d, k, d,
            )
        else:
            copy = remote(chip.at[d - 1, k], got.at[d - 1, k], d, k, d)
        copies[d, k] = copy
        copy.start()

    def stage_core(k):
        stage0[k].wait_recv()
        merge(
            chip.at[0, k], lambda s: agg[core * half + k, s], lambda s: got0[k, s], core == 1
        )
        inout[k] = jnp.zeros((2 * N, LANES), F32)
        ahead[k] = (jnp.ones((1, LANES), F32), jnp.ones((1, LANES), F32))
        chip_send(1, k)

    def stage_chip(d, k):
        copies[d, k].wait_recv()
        upper = bit[d] == 1
        from_before, from_after = ahead[k]
        theirs = got.at[d - 1, k]
        last = d == bits - 1
        inout[k, F] = inout[k, F] + jnp.where(upper, from_before, 0.0) * theirs[F]
        inout[k, B] = inout[k, B] + jnp.where(upper, 0.0, from_after) * theirs[F if last else B]
        if not last:
            ahead[k] = (
                jnp.where(upper, from_before * theirs[T1], from_before),
                jnp.where(upper, from_after, from_after * theirs[T1]),
            )
            mine = chip.at[d - 1, k]
            merge(chip.at[d, k], lambda s: mine[s], lambda s: theirs[s], upper)
            chip_send(d + 1, k)
        else:
            own = agg.at[core * half + k]
            odd = core == 1
            enter0, leave1 = inout[k, F], inout[k, B]
            low_f = jnp.where(odd, got0[k, F], own[F])
            low_t = jnp.where(odd, got0[k, T1], own[T1])
            high_b = jnp.where(odd, own[B], got0[k, B])
            high_t = jnp.where(odd, own[T1], got0[k, T1])
            enter1 = low_f + low_t * enter0
            leave0 = high_b + high_t * leave1
            final[core * half + k, F] = jnp.where(odd, enter1, enter0)
            final[core * half + k, B] = jnp.where(odd, leave1, leave0)
            other[k, F] = jnp.where(odd, enter0, enter1)
            other[k, B] = jnp.where(odd, leave0, leave1)
            copy = remote(other.at[k], final.at[core * half + k], bits, k, 0)
            copies[bits, k] = copy
            copy.start()

    mixed[...] = jnp.zeros_like(mixed)
    lane = lax.broadcasted_iota(jnp.int32, (1, LANES), 1)
    head_mask = [
        jnp.where(lane < P_SIZE, 1.0, 0.0).astype(BF16),
        jnp.where(lane < P_SIZE, 0.0, 1.0).astype(BF16),
    ]
    sub = Q // 2

    def intra(k):
        col = slice(k * LANES, (k + 1) * LANES)
        for b in range(count):
            for part_s in range(2):
                t0 = part_s * sub
                s_in = slice(part_s * sub, (part_s + 1) * sub)
                s_at = slice(b * Q + part_s * sub, b * Q + (part_s + 1) * sub)
                t_at = slice(b * Q + t0, (b + 1) * Q)
                x, u = xs[s_at, col], dy[t_at, col]
                total, mix = None, None
                for h in range(2):
                    head = 2 * k + h
                    uh = u * head_mask[h]
                    pairing = nt(x, uh)
                    within = jnp.exp2(
                        (runrow[b, head : head + 1, t0:] - colterm[b, s_in, head : head + 1])
                        + bias[b, s_in, t0:]
                    )
                    hi, lo = split2(within * scores[b, s_in, t0:])
                    product = nn(hi, uh) + nn(lo, uh)
                    total = product if total is None else total + product
                    mix = within * pairing if mix is None else mix + within * pairing
                mixed[b, s_in, t0:] += mix
                group[s_at, col] = total

    todo = {0: [("core", k) for k in range(half)]}
    for k in range(half):
        todo.setdefault(min(2 * k + 2, tiles - 1), []).append(("chip", 1, k))
    for k in range(tiles):
        intra(k)
        for task in todo.get(k, []):
            if task[0] == "core":
                stage_core(task[1])
            else:
                stage_chip(task[1], task[2])
    for b in range(count):
        blk = slice(b * Q, (b + 1) * Q)
        hi, lo = split2(mixed[b])
        part[0, blk] = nn(hi, cm[blk, :]) + nn(lo, cm[blk, :])
        hi, lo = split2(mixed[b].T)
        part[1, blk] = nn(hi, bm[blk, :]) + nn(lo, bm[blk, :])
    for d in range(2, bits):
        for k in range(half):
            stage_chip(d, k)
    for k in range(half):
        copies[bits, k].wait_recv()

    share = count * Q // hd

    def rs_copy(dest):
        return pltpu.make_async_remote_copy(
            src_ref=part.at[:, pl.ds(dest * share, share)], dst_ref=rs_got.at[row],
            send_sem=rs_send.at[dest], recv_sem=rs_recv.at[row],
            device_id={"head": dest}, device_id_type=MESH,
        )

    def state_of(b, k, forward):
        col = slice(k * LANES, (k + 1) * LANES)
        if forward:
            value = final[k, F]
            for at in range(b):
                value = local_s[at, k] + passing[at, 0:1, col] * value
        else:
            value = final[k, B]
            for at in range(count - 1, b, -1):
                value = local_a[at, k] + passing[at, 0:1, col] * value
        return split2(value)

    for b in range(count):
        blk = slice(b * Q, (b + 1) * Q)
        key, read = part[0, blk], part[1, blk]
        for k in range(tiles):
            col = slice(k * LANES, (k + 1) * LANES)
            hi, lo = state_of(b, k, False)
            x_hi = t_hi[blk, col]
            key += nt(x_hi, hi) + (nt(x_hi, lo) + nt(t_lo[blk, col], hi))
            hi, lo = state_of(b, k, True)
            y_hi = e_hi[blk, col]
            read += nt(y_hi, hi) + (nt(y_hi, lo) + nt(e_lo[blk, col], hi))
        part[0, blk] = key
        part[1, blk] = read
        for dest in range(hd):
            if b * Q < (dest + 1) * share <= (b + 1) * Q:
                @pl.when(row != dest)
                def _(dest=dest):
                    rs_copy(dest).start()
    for b in range(count):
        blk = slice(b * Q, (b + 1) * Q)
        for k in range(tiles):
            col = slice(k * LANES, (k + 1) * LANES)
            hi, lo = state_of(b, k, False)
            state_x = nn(bm[blk, :], hi) + nn(bm[blk, :], lo)
            gx_out[blk, col] = (group[blk, col] + state_x * tail_x[blk, col]).astype(BF16)
    mine = pl.ds(pl.multiple_of(row * share, share), share)
    gb_out[...] = part[0, mine]
    gc_out[...] = part[1, mine]
    for source in range(hd):
        @pl.when(row != source)
        def _(source=source):
            pltpu.make_async_remote_copy(
                src_ref=part.at[:, pl.ds(0, share)], dst_ref=rs_got.at[source],
                send_sem=rs_send.at[source], recv_sem=rs_recv.at[source],
                device_id={"head": source}, device_id_type=MESH,
            ).wait_recv()
            gb_out[...] += rs_got[source, 0]
            gc_out[...] += rs_got[source, 1]
    for dest in range(hd):
        @pl.when(row != dest)
        def _(dest=dest):
            rs_copy(dest).wait_send()
    for copy in stage0:
        copy.wait_send()
    for copy in copies.values():
        copy.wait_send()


def shards(ctx, hd, xs, bmat, cmat, logdecay, starts, output_cotangent):
    tokens, width = xs.shape
    heads = logdecay.shape[0]
    count = tokens // Q
    tiles = width // LANES
    half = tiles // 2
    bits = ctx.bit_length() - 1
    head_rows = (heads + 15) // 16 * 16
    share = tokens // hd
    packet = 2 * N + 8
    scratch = [
        pltpu.VMEM((LANES, tokens), F32),
        pltpu.VMEM((count, Q, LANES), F32),
        pltpu.VMEM((count, head_rows, Q), F32),
        pltpu.VMEM((count, 2, 3, Q, LANES), BF16),
        pltpu.VMEM((LANES, width), BF16),
        pltpu.VMEM((count, 8, width), F32),
        pltpu.VMEM((count, Q, Q), F32),
        pltpu.VMEM((count, Q, Q), F32),
        pltpu.VMEM((count, Q, Q), F32),
        pltpu.VMEM((count, N, Q), BF16),
        pltpu.VMEM((count, N, Q), BF16),
        pltpu.VMEM((tokens, width), F32),
        pltpu.VMEM((tokens, width), BF16),
        pltpu.VMEM((tokens, width), BF16),
        pltpu.VMEM((tokens, width), BF16),
        pltpu.VMEM((tokens, width), BF16),
        pltpu.VMEM((tokens, width), F32),
        pltpu.VMEM((count, tiles, N, LANES), F32),
        pltpu.VMEM((count, tiles, N, LANES), F32),
        pltpu.VMEM((tiles, packet, LANES), F32),
        pltpu.VMEM((half, packet, LANES), F32),
        pltpu.VMEM((bits - 1, half, packet, LANES), F32),
        pltpu.VMEM((bits - 1, half, packet, LANES), F32),
        pltpu.VMEM((half, 2 * N, LANES), F32),
        pltpu.VMEM((half, 2 * N, LANES), F32),
        pltpu.VMEM((tiles, 2 * N, LANES), F32),
        pltpu.VMEM((2, tokens, N), F32),
        pltpu.VMEM((hd, 2, share, N), F32),
        pltpu.SemaphoreType.DMA((bits + 1, half)),
        pltpu.SemaphoreType.DMA((bits + 1, half)),
        pltpu.SemaphoreType.DMA((hd,)),
        pltpu.SemaphoreType.DMA((hd,)),
    ]
    vmem = pl.BlockSpec(memory_space=pltpu.VMEM)
    return pl.pallas_call(
        functools.partial(kernel, ctx, hd, heads, count),
        out_shape=(
            jax.ShapeDtypeStruct((tokens, width), BF16),
            jax.ShapeDtypeStruct((share, N), F32),
            jax.ShapeDtypeStruct((share, N), F32),
        ),
        in_specs=[vmem] * 6,
        out_specs=(vmem,) * 3,
        scratch_shapes=scratch,
        compiler_params=pltpu.CompilerParams(
            collective_id=0, has_side_effects=True, vmem_limit_bytes=56 * 1024 * 1024
        ),
    )(xs, bmat, cmat, logdecay, starts.reshape(1, tokens), output_cotangent)


def solution(mesh):
    in_specs = (
        P("ctx", "head"),
        P("ctx", None),
        P("ctx", None),
        P("head", "ctx"),
        P("ctx"),
        P("ctx", "head"),
    )
    out_specs = (P("ctx", "head"), P(("ctx", "head"), None), P(("ctx", "head"), None))
    body = functools.partial(shards, mesh.shape["ctx"], mesh.shape["head"])
    return jax.shard_map(body, mesh=mesh, in_specs=in_specs, out_specs=out_specs, check_vma=False)
```

```python
import functools

import jax
import jax.numpy as jnp
from jax import lax
from jax.experimental import pallas as pl
from jax.experimental.pallas import tpu as pltpu
from jax.sharding import PartitionSpec as P

P_SIZE = 64
N = 128
Q = 256
LANES = 128
WIDE = 256
STRIDE = 32
LOG2E = 1.4426950408889634
MESH = pl.DeviceIdType.MESH
F32 = jnp.float32
BF16 = jnp.bfloat16


def nn(a, b):
    return lax.dot_general(a, b, (((1,), (0,)), ((), ())), preferred_element_type=F32)


def nt(a, b):
    return lax.dot_general(a, b, (((1,), (1,)), ((), ())), preferred_element_type=F32)


def split2(value):
    high = value.astype(BF16)
    return high, (value - high.astype(F32)).astype(BF16)


def split3(value):
    high, rest = value.astype(BF16), None
    rest = value - high.astype(F32)
    middle = rest.astype(BF16)
    return high, middle, (rest - middle.astype(F32)).astype(BF16)


def minus_expm1(x):
    series = jnp.ones_like(x)
    for term in range(11, 1, -1):
        series = 1.0 + series * x * (1.0 / term)
    return jnp.where(x > -0.5, -x * series, 1.0 - jnp.exp(x))


def kernel(
    ctx, hd, heads, count,
    xs_hbm, bm, cm, ld, st, dy_hbm,
    gx_out, gb_out, gc_out,
    xs, dy, stacked, local_sem, ldp, colterm, runrow, factor, expand, passing, bias, scores, mixed,
    keys_t, reads_t, tail_x, t_hi, t_lo, e_hi, e_lo, group, local_s, local_a,
    agg, got0, chip, got, inout, other, final, part, rs_got,
    send_sem, recv_sem, rs_send, rs_recv,
):
    width = heads * P_SIZE
    tiles = width // LANES
    half = tiles // 2
    bits = ctx.bit_length() - 1
    me, row = lax.axis_index("ctx"), lax.axis_index("head")
    bit = [(me // (1 << d)) % 2 for d in range(bits)]
    mate = [me + (1 - 2 * bit[d]) * (1 << d) for d in range(bits)]
    core = bit[0]

    loads = [
        pltpu.make_async_copy(xs_hbm, xs, local_sem.at[0]),
        pltpu.make_async_copy(dy_hbm, dy, local_sem.at[1]),
    ]
    for copy in loads:
        copy.start()
    barrier = pltpu.get_barrier_semaphore()
    for d in range(bits):
        pl.semaphore_signal(barrier, inc=1, device_id={"ctx": mate[d]}, device_id_type=MESH)
    for step in range(1, hd):
        pl.semaphore_signal(
            barrier, inc=1, device_id={"head": (row + step) % hd}, device_id_type=MESH
        )

    def remote(src, dst, stage, k, d):
        return pltpu.make_async_remote_copy(
            src_ref=src, dst_ref=dst, send_sem=send_sem.at[stage, k],
            recv_sem=recv_sem.at[stage, k], device_id={"ctx": mate[d]}, device_id_type=MESH,
        )

    rows_i = lax.broadcasted_iota(jnp.int32, (Q, Q), 0)
    cols_i = lax.broadcasted_iota(jnp.int32, (Q, Q), 1)
    tri = jnp.where(rows_i >= cols_i, 1.0, 0.0).astype(BF16)
    eye = jnp.where(rows_i == cols_i, 1.0, 0.0).astype(BF16)
    ldp[...] = jnp.zeros_like(ldp)
    for i in range(3):
        ldp[i * STRIDE : i * STRIDE + heads, :] = ld[...]
    lane = lax.broadcasted_iota(jnp.int32, (1, LANES), 1)
    er = lax.broadcasted_iota(jnp.int32, (LANES, width), 0)
    ec = lax.broadcasted_iota(jnp.int32, (LANES, width), 1)
    first = (er % STRIDE) * P_SIZE
    expand[...] = jnp.where(
        (ec >= first) & (ec < first + P_SIZE) & (er < 3 * STRIDE), 1.0, 0.0
    ).astype(BF16)

    def packed(value):
        high, middle, low = split3(value)
        rest = jnp.where(lane < 2 * STRIDE, middle.astype(F32), low.astype(F32))
        return jnp.where(lane < STRIDE, high.astype(F32), rest).astype(BF16)

    hp = runrow.shape[1]
    for b in range(count):
        blk = slice(b * Q, (b + 1) * Q)
        flags = jnp.broadcast_to(st[0:1, blk].astype(F32), (LANES, Q)).astype(BF16)
        seg_col = nt(tri, flags)
        seg_row = nt(flags[0:16], tri)
        parts = split3(ldp[:, blk])
        run = nt(tri, parts[0]) + (nt(tri, parts[1]) + nt(tri, parts[2]))
        run_r = nt(parts[0][0:hp], tri) + (nt(parts[1][0:hp], tri) + nt(parts[2][0:hp], tri))
        decay = nt(eye, parts[0]) + nt(eye, parts[1]) + nt(eye, parts[2])
        gain2 = minus_expm1(2.0 * decay)
        gain = jnp.sqrt(gain2)
        runrow[b] = run_r * LOG2E
        colterm[b] = run * LOG2E - (0.5 * LOG2E) * jnp.log(gain2)
        last, seg_last = run[Q - 1 : Q], seg_col[Q - 1 : Q]
        tail = jnp.where(seg_col == seg_last, jnp.exp(last - run), 0.0) * gain
        enter = jnp.where(seg_col == 0.0, jnp.exp(run), 0.0)
        through = jnp.broadcast_to(jnp.where(seg_last == 0.0, jnp.exp(last), 0.0), (16, LANES))
        factor[b, 0] = packed(tail)
        factor[b, 1] = packed(enter)
        passing[b] = nn(packed(through), expand[...])[0:8]
        keep = (cols_i >= rows_i) & (
            jnp.broadcast_to(seg_row[0:1], (Q, Q)) == jnp.broadcast_to(seg_col[:, 0:1], (Q, Q))
        )
        bias[b] = jnp.where(keep, 0.0, -1e30)
        keys_t[b] = nt(eye[0:N, 0:N], bm[blk, :]).astype(BF16)
        reads_t[b] = nt(eye[0:N, 0:N], cm[blk, :]).astype(BF16)
        scores[b] = nt(bm[blk, :], cm[blk, :])

    pl.semaphore_wait(barrier, bits + hd - 1)
    for copy in loads:
        copy.wait()

    def states(w):
        wide = slice(w * WIDE, (w + 1) * WIDE)
        ex = expand[:, wide]
        for b in range(count):
            blk = slice(b * Q, (b + 1) * Q)
            tx = nn(factor[b, 0], ex)
            tail_x[blk, wide] = tx
            hi, lo = split2(xs[blk, wide].astype(F32) * tx)
            t_hi[blk, wide] = hi
            t_lo[blk, wide] = lo
            own = nn(keys_t[b], hi) + nn(keys_t[b], lo)
            local_s[b, 2 * w] = own[:, :LANES]
            local_s[b, 2 * w + 1] = own[:, LANES:]
            hi, lo = split2(dy[blk, wide].astype(F32) * nn(factor[b, 1], ex))
            e_hi[blk, wide] = hi
            e_lo[blk, wide] = lo
            own = nn(reads_t[b], hi) + nn(reads_t[b], lo)
            local_a[b, 2 * w] = own[:, :LANES]
            local_a[b, 2 * w + 1] = own[:, LANES:]
        for k in (2 * w, 2 * w + 1):
            col = slice(k * LANES, (k + 1) * LANES)
            forward, backward, through = local_s[0, k], local_a[count - 1, k], passing[0, :, col]
            for b in range(1, count):
                forward = local_s[b, k] + passing[b, 0:1, col] * forward
                through = through * passing[b, :, col]
            for b in range(count - 2, -1, -1):
                backward = local_a[b, k] + passing[b, 0:1, col] * backward
            agg[k, 0:N] = forward
            agg[k, N : 2 * N] = backward
            agg[k, 2 * N : 2 * N + 8] = through

    def owned(core, k):
        return core * half + (k + (half - 1) * (1 - core)) % half

    stage0 = [remote(agg.at[owned(1 - core, k)], got0.at[k], 0, k, 0) for k in range(half)]

    F, B, T = slice(0, N), slice(N, 2 * N), slice(2 * N, 2 * N + 8)
    T1 = slice(2 * N, 2 * N + 1)
    copies = {}
    ahead = {}

    def merge(target, mine, theirs, upper):
        def low(s):
            return jnp.where(upper, theirs(s), mine(s))

        def high(s):
            return jnp.where(upper, mine(s), theirs(s))

        target[F] = high(F) + high(T1) * low(F)
        target[B] = low(B) + low(T1) * high(B)
        target[T] = low(T) * high(T)

    def chip_send(d, k):
        if d == bits - 1:
            copy = remote(
                chip.at[d - 1, k, pl.ds(pl.multiple_of(bit[d] * N, N), N)],
                got.at[d - 1, k, pl.ds(0, N)], d, k, d,
            )
        else:
            copy = remote(chip.at[d - 1, k], got.at[d - 1, k], d, k, d)
        copies[d, k] = copy
        copy.start()

    def stage_core(k):
        stage0[k].wait_recv()
        merge(
            chip.at[0, k], lambda s: agg[owned(core, k), s], lambda s: got0[k, s], core == 1
        )
        inout[k] = jnp.zeros((2 * N, LANES), F32)
        ahead[k] = (jnp.ones((1, LANES), F32), jnp.ones((1, LANES), F32))
        chip_send(1, k)

    def stage_chip(d, k):
        copies[d, k].wait_recv()
        upper = bit[d] == 1
        from_before, from_after = ahead[k]
        theirs = got.at[d - 1, k]
        last = d == bits - 1
        inout[k, F] = inout[k, F] + jnp.where(upper, from_before, 0.0) * theirs[F]
        inout[k, B] = inout[k, B] + jnp.where(upper, 0.0, from_after) * theirs[F if last else B]
        if not last:
            ahead[k] = (
                jnp.where(upper, from_before * theirs[T1], from_before),
                jnp.where(upper, from_after, from_after * theirs[T1]),
            )
            mine = chip.at[d - 1, k]
            merge(chip.at[d, k], lambda s: mine[s], lambda s: theirs[s], upper)
            chip_send(d + 1, k)
        else:
            own = agg.at[owned(core, k)]
            odd = core == 1
            enter0, leave1 = inout[k, F], inout[k, B]
            low_f = jnp.where(odd, got0[k, F], own[F])
            low_t = jnp.where(odd, got0[k, T1], own[T1])
            high_b = jnp.where(odd, own[B], got0[k, B])
            high_t = jnp.where(odd, own[T1], got0[k, T1])
            enter1 = low_f + low_t * enter0
            leave0 = high_b + high_t * leave1
            final[owned(core, k), F] = jnp.where(odd, enter1, enter0)
            final[owned(core, k), B] = jnp.where(odd, leave1, leave0)
            other[k, F] = jnp.where(odd, enter0, enter1)
            other[k, B] = jnp.where(odd, leave0, leave1)
            copy = remote(other.at[k], final.at[owned(core, k)], bits, k, 0)
            copies[bits, k] = copy
            copy.start()

    mixed[...] = jnp.zeros_like(mixed)
    head_mask = [
        jnp.where(lane < P_SIZE, 1.0, 0.0).astype(BF16),
        jnp.where(lane < P_SIZE, 0.0, 1.0).astype(BF16),
    ]
    sub = Q // 2

    def intra(k):
        col = slice(k * LANES, (k + 1) * LANES)
        for b in range(count):
            for part_s in range(2):
                t0 = part_s * sub
                s_in = slice(part_s * sub, (part_s + 1) * sub)
                s_at = slice(b * Q + part_s * sub, b * Q + (part_s + 1) * sub)
                t_at = slice(b * Q + t0, (b + 1) * Q)
                x, u = xs[s_at, col], dy[t_at, col]
                total, mix = None, None
                for h in range(2):
                    head = 2 * k + h
                    uh = u * head_mask[h]
                    pairing = nt(x, uh)
                    within = jnp.exp2(
                        (runrow[b, head : head + 1, t0:] - colterm[b, s_in, head : head + 1])
                        + bias[b, s_in, t0:]
                    )
                    hi, lo = split2(within * scores[b, s_in, t0:])
                    product = nn(hi, uh) + nn(lo, uh)
                    total = product if total is None else total + product
                    mix = within * pairing if mix is None else mix + within * pairing
                mixed[b, s_in, t0:] += mix
                group[s_at, col] = total

    wides = width // WIDE
    middle = wides // 2
    states(middle)
    stage0[0].start()
    for w in range(middle):
        states(w)
        states(middle + 1 + w)
        for k in (2 * w + 1, 2 * w + 2):
            stage0[k].start()
        for k in range(max(0, 2 * w - 1), 2 * w + 1):
            stage_core(k)
    intra(0)
    for k in range(half - 2, half):
        stage_core(k)
    todo = {}
    for k in range(half):
        todo.setdefault(min(2 * k + 2, tiles - 1), []).append((1, k))
    for k in range(1, tiles):
        intra(k)
        for d, at in todo.get(k, []):
            stage_chip(d, at)
    for b in range(count):
        blk = slice(b * Q, (b + 1) * Q)
        hi, lo = split2(mixed[b])
        part[0, blk] = nn(hi, cm[blk, :]) + nn(lo, cm[blk, :])
        hi, lo = split2(mixed[b].T)
        part[1, blk] = nn(hi, bm[blk, :]) + nn(lo, bm[blk, :])
    for d in range(2, bits):
        for k in range(half):
            stage_chip(d, k)
    for k in range(half):
        copies[bits, k].wait_recv()

    share = count * Q // hd

    def rs_copy(dest):
        return pltpu.make_async_remote_copy(
            src_ref=part.at[:, pl.ds(dest * share, share)], dst_ref=rs_got.at[row],
            send_sem=rs_send.at[dest], recv_sem=rs_recv.at[row],
            device_id={"head": dest}, device_id_type=MESH,
        )

    def state_of(b, w, forward):
        wide = slice(w * WIDE, (w + 1) * WIDE)
        rows, chain = (F, range(b)) if forward else (B, range(count - 1, b, -1))
        local = local_s if forward else local_a
        value = jnp.concatenate([final[2 * w, rows], final[2 * w + 1, rows]], axis=1)
        for at in chain:
            value = (
                jnp.concatenate([local[at, 2 * w], local[at, 2 * w + 1]], axis=1)
                + passing[at, 0:1, wide] * value
            )
        return jnp.concatenate(split2(value), axis=0)

    for b in range(count):
        blk = slice(b * Q, (b + 1) * Q)
        key, read, key2, read2 = part[0, blk], part[1, blk], None, None
        for w in range(wides):
            wide = slice(w * WIDE, (w + 1) * WIDE)
            both = state_of(b, w, False)
            stacked[b, w] = both
            product = nt(t_hi[blk, wide], both)
            key2 = product if w == 0 else key2 + product
            key += nt(t_lo[blk, wide], both[0:N])
            both = state_of(b, w, True)
            product = nt(e_hi[blk, wide], both)
            read2 = product if w == 0 else read2 + product
            read += nt(e_lo[blk, wide], both[0:N])
        part[0, blk] = key + (key2[:, :N] + key2[:, N:])
        part[1, blk] = read + (read2[:, :N] + read2[:, N:])
        for dest in range(hd):
            if b * Q < (dest + 1) * share <= (b + 1) * Q:
                @pl.when(row != dest)
                def _(dest=dest):
                    rs_copy(dest).start()
    for b in range(count):
        blk = slice(b * Q, (b + 1) * Q)
        keys2 = jnp.concatenate([bm[blk, :], bm[blk, :]], axis=1)
        for w in range(wides):
            wide = slice(w * WIDE, (w + 1) * WIDE)
            state_x = nn(keys2, stacked[b, w])
            gx_out[blk, wide] = (group[blk, wide] + state_x * tail_x[blk, wide]).astype(BF16)
    mine = pl.ds(pl.multiple_of(row * share, share), share)
    gb_out[...] = part[0, mine]
    gc_out[...] = part[1, mine]
    for source in range(hd):
        @pl.when(row != source)
        def _(source=source):
            pltpu.make_async_remote_copy(
                src_ref=part.at[:, pl.ds(0, share)], dst_ref=rs_got.at[source],
                send_sem=rs_send.at[source], recv_sem=rs_recv.at[source],
                device_id={"head": source}, device_id_type=MESH,
            ).wait_recv()
            gb_out[...] += rs_got[source, 0]
            gc_out[...] += rs_got[source, 1]
    for dest in range(hd):
        @pl.when(row != dest)
        def _(dest=dest):
            rs_copy(dest).wait_send()
    for copy in stage0:
        copy.wait_send()
    for copy in copies.values():
        copy.wait_send()


def shards(ctx, hd, xs, bmat, cmat, logdecay, starts, output_cotangent):
    tokens, width = xs.shape
    heads = logdecay.shape[0]
    count = tokens // Q
    tiles = width // LANES
    half = tiles // 2
    bits = ctx.bit_length() - 1
    head_rows = (heads + 15) // 16 * 16
    share = tokens // hd
    packet = 2 * N + 8
    scratch = [
        pltpu.VMEM((tokens, width), BF16),
        pltpu.VMEM((tokens, width), BF16),
        pltpu.VMEM((count, width // WIDE, 2 * N, WIDE), BF16),
        pltpu.SemaphoreType.DMA((2 + count,)),
        pltpu.VMEM((LANES, tokens), F32),
        pltpu.VMEM((count, Q, LANES), F32),
        pltpu.VMEM((count, head_rows, Q), F32),
        pltpu.VMEM((count, 2, Q, LANES), BF16),
        pltpu.VMEM((LANES, width), BF16),
        pltpu.VMEM((count, 8, width), F32),
        pltpu.VMEM((count, Q, Q), F32),
        pltpu.VMEM((count, Q, Q), F32),
        pltpu.VMEM((count, Q, Q), F32),
        pltpu.VMEM((count, N, Q), BF16),
        pltpu.VMEM((count, N, Q), BF16),
        pltpu.VMEM((tokens, width), F32),
        pltpu.VMEM((tokens, width), BF16),
        pltpu.VMEM((tokens, width), BF16),
        pltpu.VMEM((tokens, width), BF16),
        pltpu.VMEM((tokens, width), BF16),
        pltpu.VMEM((tokens, width), F32),
        pltpu.VMEM((count, tiles, N, LANES), F32),
        pltpu.VMEM((count, tiles, N, LANES), F32),
        pltpu.VMEM((tiles, packet, LANES), F32),
        pltpu.VMEM((half, packet, LANES), F32),
        pltpu.VMEM((bits - 1, half, packet, LANES), F32),
        pltpu.VMEM((bits - 1, half, packet, LANES), F32),
        pltpu.VMEM((half, 2 * N, LANES), F32),
        pltpu.VMEM((half, 2 * N, LANES), F32),
        pltpu.VMEM((tiles, 2 * N, LANES), F32),
        pltpu.VMEM((2, tokens, N), F32),
        pltpu.VMEM((hd, 2, share, N), F32),
        pltpu.SemaphoreType.DMA((bits + 1, half)),
        pltpu.SemaphoreType.DMA((bits + 1, half)),
        pltpu.SemaphoreType.DMA((hd,)),
        pltpu.SemaphoreType.DMA((hd,)),
    ]
    vmem = pl.BlockSpec(memory_space=pltpu.VMEM)
    anywhere = pl.BlockSpec(memory_space=pl.ANY)
    results = pl.pallas_call(
        functools.partial(kernel, ctx, hd, heads, count),
        out_shape=(
            pltpu.VMEM((tokens, width), BF16),
            pltpu.VMEM((share, N), F32),
            pltpu.VMEM((share, N), F32),
        ),
        in_specs=[anywhere, vmem, vmem, vmem, vmem, anywhere],
        out_specs=(vmem, vmem, vmem),
        scratch_shapes=scratch,
        compiler_params=pltpu.CompilerParams(
            collective_id=0, has_side_effects=True, vmem_limit_bytes=56 * 1024 * 1024
        ),
    )(xs, bmat, cmat, logdecay, starts.reshape(1, tokens), output_cotangent)
    return results


def solution(mesh):
    in_specs = (
        P("ctx", "head"),
        P("ctx", None),
        P("ctx", None),
        P("head", "ctx"),
        P("ctx"),
        P("ctx", "head"),
    )
    out_specs = (P("ctx", "head"), P(("ctx", "head"), None), P(("ctx", "head"), None))
    body = functools.partial(shards, mesh.shape["ctx"], mesh.shape["head"])
    return jax.shard_map(body, mesh=mesh, in_specs=in_specs, out_specs=out_specs, check_vma=False)
```

```python
import functools

import jax
import jax.numpy as jnp
from jax import lax
from jax.experimental import pallas as pl
from jax.experimental.pallas import tpu as pltpu
from jax.sharding import PartitionSpec as P

P_SIZE = 64
N = 128
Q = 256
LANES = 128
WIDE = 256
STRIDE = 32
LOG2E = 1.4426950408889634
MESH = pl.DeviceIdType.MESH
F32 = jnp.float32
BF16 = jnp.bfloat16


def nn(a, b):
    return lax.dot_general(a, b, (((1,), (0,)), ((), ())), preferred_element_type=F32)


def nt(a, b):
    return lax.dot_general(a, b, (((1,), (1,)), ((), ())), preferred_element_type=F32)


def split2(value):
    high = value.astype(BF16)
    return high, (value - high.astype(F32)).astype(BF16)


def split3(value):
    high, rest = value.astype(BF16), None
    rest = value - high.astype(F32)
    middle = rest.astype(BF16)
    return high, middle, (rest - middle.astype(F32)).astype(BF16)


def minus_expm1(x):
    series = jnp.ones_like(x)
    for term in range(11, 1, -1):
        series = 1.0 + series * x * (1.0 / term)
    return jnp.where(x > -0.5, -x * series, 1.0 - jnp.exp(x))


def kernel(
    ctx, hd, heads, count,
    xs_hbm, bm, cm, ld, st, dy_hbm,
    gx_out, gb_out, gc_out,
    xs, dy, stacked, local_sem, more, pair, across, ldp, colterm, runrow, factor, expand, passing, bias, scores, mixed,
    keys_t, reads_t, tail_x, t_hi, t_lo, e_hi, e_lo, group, local_s, local_a,
    agg, got0, chip, got, inout, other, final, part, rs_got,
    send_sem, recv_sem, rs_send, rs_recv,
):
    width = heads * P_SIZE
    tiles = width // LANES
    half = tiles // 2
    bits = ctx.bit_length() - 1
    me, row = lax.axis_index("ctx"), lax.axis_index("head")
    bit = [(me // (1 << d)) % 2 for d in range(bits)]
    mate = [me + (1 - 2 * bit[d]) * (1 << d) for d in range(bits)]
    core = bit[0]

    loads = [
        pltpu.make_async_copy(xs_hbm, xs, local_sem.at[0]),
        pltpu.make_async_copy(dy_hbm, dy, local_sem.at[1]),
    ]
    for copy in loads:
        copy.start()
    barrier = pltpu.get_barrier_semaphore()
    for d in range(bits):
        pl.semaphore_signal(barrier, inc=1, device_id={"ctx": mate[d]}, device_id_type=MESH)
    for step in range(1, hd):
        pl.semaphore_signal(
            barrier, inc=1, device_id={"head": (row + step) % hd}, device_id_type=MESH
        )

    def remote(src, dst, stage, k, d):
        return pltpu.make_async_remote_copy(
            src_ref=src, dst_ref=dst, send_sem=send_sem.at[stage, k],
            recv_sem=recv_sem.at[stage, k], device_id={"ctx": mate[d]}, device_id_type=MESH,
        )

    rows_i = lax.broadcasted_iota(jnp.int32, (Q, Q), 0)
    cols_i = lax.broadcasted_iota(jnp.int32, (Q, Q), 1)
    tri = jnp.where(rows_i >= cols_i, 1.0, 0.0).astype(BF16)
    eye = jnp.where(rows_i == cols_i, 1.0, 0.0).astype(BF16)
    ldp[...] = jnp.zeros_like(ldp)
    for i in range(3):
        ldp[i * STRIDE : i * STRIDE + heads, :] = ld[...]
    lane = lax.broadcasted_iota(jnp.int32, (1, LANES), 1)
    er = lax.broadcasted_iota(jnp.int32, (LANES, width), 0)
    ec = lax.broadcasted_iota(jnp.int32, (LANES, width), 1)
    first = (er % STRIDE) * P_SIZE
    expand[...] = jnp.where(
        (ec >= first) & (ec < first + P_SIZE) & (er < 3 * STRIDE), 1.0, 0.0
    ).astype(BF16)

    def packed(value):
        high, middle, low = split3(value)
        rest = jnp.where(lane < 2 * STRIDE, middle.astype(F32), low.astype(F32))
        return jnp.where(lane < STRIDE, high.astype(F32), rest).astype(BF16)

    hp = runrow.shape[1]
    for b in range(count):
        blk = slice(b * Q, (b + 1) * Q)
        flags = jnp.broadcast_to(st[0:1, blk].astype(F32), (LANES, Q)).astype(BF16)
        seg_col = nt(tri, flags)
        seg_row = nt(flags[0:16], tri)
        parts = split3(ldp[:, blk])
        run = nt(tri, parts[0]) + (nt(tri, parts[1]) + nt(tri, parts[2]))
        run_r = nt(parts[0][0:hp], tri) + (nt(parts[1][0:hp], tri) + nt(parts[2][0:hp], tri))
        decay = nt(eye, parts[0]) + nt(eye, parts[1]) + nt(eye, parts[2])
        gain2 = minus_expm1(2.0 * decay)
        gain = jnp.sqrt(gain2)
        runrow[b] = run_r * LOG2E
        colterm[b] = run * LOG2E - (0.5 * LOG2E) * jnp.log(gain2)
        last, seg_last = run[Q - 1 : Q], seg_col[Q - 1 : Q]
        tail = jnp.where(seg_col == seg_last, jnp.exp(last - run), 0.0) * gain
        enter = jnp.where(seg_col == 0.0, jnp.exp(run), 0.0)
        through = jnp.broadcast_to(jnp.where(seg_last == 0.0, jnp.exp(last), 0.0), (16, LANES))
        factor[b, 0] = packed(tail)
        factor[b, 1] = packed(enter)
        passing[b] = nn(packed(through), expand[...])[0:8]
        keep = (cols_i >= rows_i) & (
            jnp.broadcast_to(seg_row[0:1], (Q, Q)) == jnp.broadcast_to(seg_col[:, 0:1], (Q, Q))
        )
        bias[b] = jnp.where(keep, 0.0, -1e30)
        keys_t[b] = nt(eye[0:N, 0:N], bm[blk, :]).astype(BF16)
        reads_t[b] = nt(eye[0:N, 0:N], cm[blk, :]).astype(BF16)
        scores[b] = nt(bm[blk, :], cm[blk, :])

    pl.semaphore_wait(barrier, bits + hd - 1)
    for copy in loads:
        copy.wait()

    F, T, T1 = slice(0, N), slice(N, N + 8), slice(N, N + 1)
    B, TB = slice(N + 8, 2 * N + 8), slice(2 * N + 8, 2 * N + 16)
    portion = N + 8

    def states(w):
        wide = slice(w * WIDE, (w + 1) * WIDE)
        ex = expand[:, wide]
        for b in range(count):
            blk = slice(b * Q, (b + 1) * Q)
            tx = nn(factor[b, 0], ex)
            tail_x[blk, wide] = tx
            hi, lo = split2(xs[blk, wide].astype(F32) * tx)
            t_hi[blk, wide] = hi
            t_lo[blk, wide] = lo
            own = nn(keys_t[b], hi) + nn(keys_t[b], lo)
            local_s[b, 2 * w] = own[:, :LANES]
            local_s[b, 2 * w + 1] = own[:, LANES:]
            hi, lo = split2(dy[blk, wide].astype(F32) * nn(factor[b, 1], ex))
            e_hi[blk, wide] = hi
            e_lo[blk, wide] = lo
            own = nn(reads_t[b], hi) + nn(reads_t[b], lo)
            local_a[b, 2 * w] = own[:, :LANES]
            local_a[b, 2 * w + 1] = own[:, LANES:]
        for k in (2 * w, 2 * w + 1):
            col = slice(k * LANES, (k + 1) * LANES)
            forward, backward, through = local_s[0, k], local_a[count - 1, k], passing[0, :, col]
            for b in range(1, count):
                forward = local_s[b, k] + passing[b, 0:1, col] * forward
                through = through * passing[b, :, col]
            for b in range(count - 2, -1, -1):
                backward = local_a[b, k] + passing[b, 0:1, col] * backward
            agg[k, F] = forward
            agg[k, T] = through
            agg[k, B] = backward
            agg[k, TB] = through

    def owned(core, k):
        return core * half + (k + (half - 1) * (1 - core)) % half

    stage0 = [remote(agg.at[owned(1 - core, k)], got0.at[k], 0, k, 0) for k in range(half)]

    I, O = slice(0, N), slice(N, 2 * N)
    forwarded = 2
    copies = {}
    ahead = {}

    def merge(target, mine, theirs, upper):
        def low(s):
            return jnp.where(upper, theirs(s), mine(s))

        def high(s):
            return jnp.where(upper, mine(s), theirs(s))

        target[F] = high(F) + high(T1) * low(F)
        target[B] = low(B) + low(T1) * high(B)
        through = low(T) * high(T)
        target[T] = through
        target[TB] = through

    near, far = bits - 2, bits - 1
    lo_bit, hi_bit = bit[near], bit[far]
    inner = lo_bit + hi_bit == 1
    outer = lo_bit + hi_bit != 1
    started = []

    def begin(copy, condition=None):
        started.append((copy, condition))
        guarded(copy.start, condition)
        return copy

    def guarded(action, condition):
        if condition is None:
            action()
        else:
            pl.when(condition)(action)

    def chip_send(d, k):
        if d < near:
            copies[d, k] = begin(remote(chip.at[d - 1, k], got.at[d - 1, k], d, k, d))
            return
        source = chip.at[d - 1, k]
        copies["near", k] = begin(remote(
            source.at[pl.ds(pl.multiple_of(lo_bit * portion, 8), portion)],
            got.at[d - 1, k, pl.ds(0, portion)], near, k, near,
        ))
        if k >= forwarded:
            copies["more", k] = begin(remote(
                source.at[pl.ds(pl.multiple_of((1 - lo_bit) * portion, 8), N)],
                more.at[k], bits + 1, k, near,
            ), inner)

    def stage_core(k):
        stage0[k].wait_recv()
        merge(
            chip.at[0, k], lambda s: agg[owned(core, k), s], lambda s: got0[k, s], core == 1
        )
        inout[k] = jnp.zeros((2 * N, LANES), F32)
        ahead[k] = (jnp.ones((1, LANES), F32), jnp.ones((1, LANES), F32))
        chip_send(1, k)

    def stage_chip(d, k):
        copies[d, k].wait_recv()
        upper = bit[d] == 1
        from_before, from_after = ahead[k]
        theirs, mine = got.at[d - 1, k], chip.at[d - 1, k]
        inout[k, I] = inout[k, I] + jnp.where(upper, from_before, 0.0) * theirs[F]
        inout[k, O] = inout[k, O] + jnp.where(upper, 0.0, from_after) * theirs[B]
        ahead[k] = (
            jnp.where(upper, from_before * theirs[T1], from_before),
            jnp.where(upper, from_after, from_after * theirs[T1]),
        )
        merge(chip.at[d, k], lambda s: mine[s], lambda s: theirs[s], upper)
        chip_send(d + 1, k)

    def stage_near(k):
        copies["near", k].wait_recv()
        theirs, mine = got.at[near - 1, k], chip.at[near - 1, k]
        own = jnp.where(hi_bit == 0, mine[F], mine[B])
        both = own + mine[T1] * theirs[F]
        if k >= forwarded:
            guarded(copies["more", k].wait_recv, outer)
            both = jnp.where(inner, both, more[k] + theirs[T1] * own)
        pair[k] = both
        copies["far", k] = begin(
            remote(pair.at[k], across.at[k], far, k, far), inner if k < forwarded else None
        )

    def stage_forward(k):
        guarded(copies["far", k].wait_recv, outer)
        copies["on", k] = begin(remote(across.at[k], across.at[k], bits + 2, k, near), outer)

    def stage_far(k):
        if k < forwarded:
            guarded(copies["on", k].wait_recv, inner)
        else:
            copies["far", k].wait_recv()
        theirs, beyond = got.at[near - 1, k], across[k]
        near_side = jnp.where(inner, theirs[F], theirs[F] + theirs[T1] * beyond)
        from_before, from_after = ahead[k]
        far_before = jnp.where(hi_bit == 1, beyond, 0.0)
        far_after = jnp.where(hi_bit == 0, beyond, 0.0)
        enter0 = inout[k, I] + from_before * jnp.where(lo_bit == 1, near_side, far_before)
        leave1 = inout[k, O] + from_after * jnp.where(lo_bit == 0, near_side, far_after)
        own = agg.at[owned(core, k)]
        odd = core == 1
        low_f = jnp.where(odd, got0[k, F], own[F])
        low_t = jnp.where(odd, got0[k, T1], own[T1])
        high_b = jnp.where(odd, own[B], got0[k, B])
        high_t = jnp.where(odd, own[T1], got0[k, T1])
        enter1 = low_f + low_t * enter0
        leave0 = high_b + high_t * leave1
        final[owned(core, k), I] = jnp.where(odd, enter1, enter0)
        final[owned(core, k), O] = jnp.where(odd, leave1, leave0)
        other[k, I] = jnp.where(odd, enter0, enter1)
        other[k, O] = jnp.where(odd, leave0, leave1)
        copies["core", k] = begin(remote(other.at[k], final.at[owned(core, k)], bits, k, 0))

    mixed[...] = jnp.zeros_like(mixed)
    head_mask = [
        jnp.where(lane < P_SIZE, 1.0, 0.0).astype(BF16),
        jnp.where(lane < P_SIZE, 0.0, 1.0).astype(BF16),
    ]
    sub = Q // 2

    def intra(k):
        col = slice(k * LANES, (k + 1) * LANES)
        for b in range(count):
            for part_s in range(2):
                t0 = part_s * sub
                s_in = slice(part_s * sub, (part_s + 1) * sub)
                s_at = slice(b * Q + part_s * sub, b * Q + (part_s + 1) * sub)
                t_at = slice(b * Q + t0, (b + 1) * Q)
                x, u = xs[s_at, col], dy[t_at, col]
                total, mix = None, None
                for h in range(2):
                    head = 2 * k + h
                    uh = u * head_mask[h]
                    pairing = nt(x, uh)
                    within = jnp.exp2(
                        (runrow[b, head : head + 1, t0:] - colterm[b, s_in, head : head + 1])
                        + bias[b, s_in, t0:]
                    )
                    hi, lo = split2(within * scores[b, s_in, t0:])
                    product = nn(hi, uh) + nn(lo, uh)
                    total = product if total is None else total + product
                    mix = within * pairing if mix is None else mix + within * pairing
                mixed[b, s_in, t0:] += mix
                group[s_at, col] = total

    wides = width // WIDE
    middle = wides // 2
    states(middle)
    stage0[0].start()
    for w in range(middle):
        states(w)
        states(middle + 1 + w)
        for k in (2 * w + 1, 2 * w + 2):
            stage0[k].start()
        for k in range(max(0, 2 * w - 1), 2 * w + 1):
            stage_core(k)
    intra(0)
    for k in range(half - 2, half):
        stage_core(k)
    for k in range(1, tiles):
        intra(k)
        if near == 1 and k in (4, 7):
            stage_near(0 if k == 4 else 1)
    for b in range(count):
        blk = slice(b * Q, (b + 1) * Q)
        hi, lo = split2(mixed[b])
        part[0, blk] = nn(hi, cm[blk, :]) + nn(lo, cm[blk, :])
        hi, lo = split2(mixed[b].T)
        part[1, blk] = nn(hi, bm[blk, :]) + nn(lo, bm[blk, :])
    for d in range(1, near):
        for k in range(half):
            stage_chip(d, k)
    if near > 1:
        for k in range(forwarded):
            stage_near(k)
    for k in range(forwarded):
        stage_forward(k)
    stage_near(2)
    for k in range(forwarded):
        stage_far(k)
    for k in range(3, half):
        stage_near(k)
        stage_far(k - 1)
    stage_far(half - 1)
    for k in range(half):
        copies["core", k].wait_recv()

    share = count * Q // hd

    def rs_copy(dest):
        return pltpu.make_async_remote_copy(
            src_ref=part.at[:, pl.ds(dest * share, share)], dst_ref=rs_got.at[row],
            send_sem=rs_send.at[dest], recv_sem=rs_recv.at[row],
            device_id={"head": dest}, device_id_type=MESH,
        )

    def state_of(b, w, forward):
        wide = slice(w * WIDE, (w + 1) * WIDE)
        rows, chain = (I, range(b)) if forward else (O, range(count - 1, b, -1))
        local = local_s if forward else local_a
        value = jnp.concatenate([final[2 * w, rows], final[2 * w + 1, rows]], axis=1)
        for at in chain:
            value = (
                jnp.concatenate([local[at, 2 * w], local[at, 2 * w + 1]], axis=1)
                + passing[at, 0:1, wide] * value
            )
        return jnp.concatenate(split2(value), axis=0)

    for b in range(count):
        blk = slice(b * Q, (b + 1) * Q)
        key, read, key2, read2 = part[0, blk], part[1, blk], None, None
        for w in range(wides):
            wide = slice(w * WIDE, (w + 1) * WIDE)
            both = state_of(b, w, False)
            stacked[b, w] = both
            product = nt(t_hi[blk, wide], both)
            key2 = product if w == 0 else key2 + product
            key += nt(t_lo[blk, wide], both[0:N])
            both = state_of(b, w, True)
            product = nt(e_hi[blk, wide], both)
            read2 = product if w == 0 else read2 + product
            read += nt(e_lo[blk, wide], both[0:N])
        part[0, blk] = key + (key2[:, :N] + key2[:, N:])
        part[1, blk] = read + (read2[:, :N] + read2[:, N:])
        for dest in range(hd):
            if b * Q < (dest + 1) * share <= (b + 1) * Q:
                @pl.when(row != dest)
                def _(dest=dest):
                    rs_copy(dest).start()
    for b in range(count):
        blk = slice(b * Q, (b + 1) * Q)
        keys2 = jnp.concatenate([bm[blk, :], bm[blk, :]], axis=1)
        for w in range(wides):
            wide = slice(w * WIDE, (w + 1) * WIDE)
            state_x = nn(keys2, stacked[b, w])
            gx_out[blk, wide] = (group[blk, wide] + state_x * tail_x[blk, wide]).astype(BF16)
    mine = pl.ds(pl.multiple_of(row * share, share), share)
    gb_out[...] = part[0, mine]
    gc_out[...] = part[1, mine]
    for source in range(hd):
        @pl.when(row != source)
        def _(source=source):
            pltpu.make_async_remote_copy(
                src_ref=part.at[:, pl.ds(0, share)], dst_ref=rs_got.at[source],
                send_sem=rs_send.at[source], recv_sem=rs_recv.at[source],
                device_id={"head": source}, device_id_type=MESH,
            ).wait_recv()
            gb_out[...] += rs_got[source, 0]
            gc_out[...] += rs_got[source, 1]
    for dest in range(hd):
        @pl.when(row != dest)
        def _(dest=dest):
            rs_copy(dest).wait_send()
    for copy in stage0:
        copy.wait_send()
    for copy, condition in started:
        guarded(copy.wait_send, condition)


def shards(ctx, hd, xs, bmat, cmat, logdecay, starts, output_cotangent):
    tokens, width = xs.shape
    heads = logdecay.shape[0]
    count = tokens // Q
    tiles = width // LANES
    half = tiles // 2
    bits = ctx.bit_length() - 1
    head_rows = (heads + 15) // 16 * 16
    share = tokens // hd
    packet = 2 * N + 16
    scratch = [
        pltpu.VMEM((tokens, width), BF16),
        pltpu.VMEM((tokens, width), BF16),
        pltpu.VMEM((count, width // WIDE, 2 * N, WIDE), BF16),
        pltpu.SemaphoreType.DMA((2,)),
        pltpu.VMEM((half, N, LANES), F32),
        pltpu.VMEM((half, N, LANES), F32),
        pltpu.VMEM((half, N, LANES), F32),
        pltpu.VMEM((LANES, tokens), F32),
        pltpu.VMEM((count, Q, LANES), F32),
        pltpu.VMEM((count, head_rows, Q), F32),
        pltpu.VMEM((count, 2, Q, LANES), BF16),
        pltpu.VMEM((LANES, width), BF16),
        pltpu.VMEM((count, 8, width), F32),
        pltpu.VMEM((count, Q, Q), F32),
        pltpu.VMEM((count, Q, Q), F32),
        pltpu.VMEM((count, Q, Q), F32),
        pltpu.VMEM((count, N, Q), BF16),
        pltpu.VMEM((count, N, Q), BF16),
        pltpu.VMEM((tokens, width), F32),
        pltpu.VMEM((tokens, width), BF16),
        pltpu.VMEM((tokens, width), BF16),
        pltpu.VMEM((tokens, width), BF16),
        pltpu.VMEM((tokens, width), BF16),
        pltpu.VMEM((tokens, width), F32),
        pltpu.VMEM((count, tiles, N, LANES), F32),
        pltpu.VMEM((count, tiles, N, LANES), F32),
        pltpu.VMEM((tiles, packet, LANES), F32),
        pltpu.VMEM((half, packet, LANES), F32),
        pltpu.VMEM((bits - 1, half, packet, LANES), F32),
        pltpu.VMEM((bits - 1, half, packet, LANES), F32),
        pltpu.VMEM((half, 2 * N, LANES), F32),
        pltpu.VMEM((half, 2 * N, LANES), F32),
        pltpu.VMEM((tiles, 2 * N, LANES), F32),
        pltpu.VMEM((2, tokens, N), F32),
        pltpu.VMEM((hd, 2, share, N), F32),
        pltpu.SemaphoreType.DMA((bits + 3, half)),
        pltpu.SemaphoreType.DMA((bits + 3, half)),
        pltpu.SemaphoreType.DMA((hd,)),
        pltpu.SemaphoreType.DMA((hd,)),
    ]
    vmem = pl.BlockSpec(memory_space=pltpu.VMEM)
    anywhere = pl.BlockSpec(memory_space=pl.ANY)
    results = pl.pallas_call(
        functools.partial(kernel, ctx, hd, heads, count),
        out_shape=(
            pltpu.VMEM((tokens, width), BF16),
            pltpu.VMEM((share, N), F32),
            pltpu.VMEM((share, N), F32),
        ),
        in_specs=[anywhere, vmem, vmem, vmem, vmem, anywhere],
        out_specs=(vmem, vmem, vmem),
        scratch_shapes=scratch,
        compiler_params=pltpu.CompilerParams(
            collective_id=0, has_side_effects=True, vmem_limit_bytes=56 * 1024 * 1024
        ),
    )(xs, bmat, cmat, logdecay, starts.reshape(1, tokens), output_cotangent)
    return results


def solution(mesh):
    in_specs = (
        P("ctx", "head"),
        P("ctx", None),
        P("ctx", None),
        P("head", "ctx"),
        P("ctx"),
        P("ctx", "head"),
    )
    out_specs = (P("ctx", "head"), P(("ctx", "head"), None), P(("ctx", "head"), None))
    body = functools.partial(shards, mesh.shape["ctx"], mesh.shape["head"])
    return jax.shard_map(body, mesh=mesh, in_specs=in_specs, out_specs=out_specs, check_vma=False)
```

```python
import functools

import jax
import jax.numpy as jnp
from jax import lax
from jax.experimental import pallas as pl
from jax.experimental.pallas import tpu as pltpu
from jax.sharding import PartitionSpec as P

P_SIZE = 64
N = 128
Q = 256
LANES = 128
WIDE = 256
STRIDE = 32
LOG2E = 1.4426950408889634
MESH = pl.DeviceIdType.MESH
F32 = jnp.float32
BF16 = jnp.bfloat16


def nn(a, b):
    return lax.dot_general(a, b, (((1,), (0,)), ((), ())), preferred_element_type=F32)


def nt(a, b):
    return lax.dot_general(a, b, (((1,), (1,)), ((), ())), preferred_element_type=F32)


def split2(value):
    high = value.astype(BF16)
    return high, (value - high.astype(F32)).astype(BF16)


def split3(value):
    high, rest = value.astype(BF16), None
    rest = value - high.astype(F32)
    middle = rest.astype(BF16)
    return high, middle, (rest - middle.astype(F32)).astype(BF16)


def minus_expm1(x):
    series = jnp.ones_like(x)
    for term in range(11, 1, -1):
        series = 1.0 + series * x * (1.0 / term)
    return jnp.where(x > -0.5, -x * series, 1.0 - jnp.exp(x))


def kernel(
    ctx, hd, heads, count,
    xs_hbm, bm, cm, ld, st, dy_hbm,
    gx_out, gb_out, gc_out,
    xs, dy, stacked, local_sem, more, pair, across, sums, ldp, colterm, runrow, factor, expand, passing, bias, scores, mixed,
    keys_t, reads_t, tail_x, t_hi, t_lo, e_hi, e_lo, group, local_s, local_a,
    agg, got0, chip, got, inout, other, final, part, rs_got,
    send_sem, recv_sem, rs_send, rs_recv,
):
    width = heads * P_SIZE
    tiles = width // LANES
    half = tiles // 2
    bits = ctx.bit_length() - 1
    me, row = lax.axis_index("ctx"), lax.axis_index("head")
    bit = [(me // (1 << d)) % 2 for d in range(bits)]
    mate = [me + (1 - 2 * bit[d]) * (1 << d) for d in range(bits)]
    core = bit[0]

    loads = [
        pltpu.make_async_copy(xs_hbm, xs, local_sem.at[0]),
        pltpu.make_async_copy(dy_hbm, dy, local_sem.at[1]),
    ]
    for copy in loads:
        copy.start()
    barrier = pltpu.get_barrier_semaphore()
    for d in range(bits):
        pl.semaphore_signal(barrier, inc=1, device_id={"ctx": mate[d]}, device_id_type=MESH)
    for step in range(1, hd):
        pl.semaphore_signal(
            barrier, inc=1, device_id={"head": (row + step) % hd}, device_id_type=MESH
        )

    def remote(src, dst, stage, k, d):
        return pltpu.make_async_remote_copy(
            src_ref=src, dst_ref=dst, send_sem=send_sem.at[stage, k],
            recv_sem=recv_sem.at[stage, k], device_id={"ctx": mate[d]}, device_id_type=MESH,
        )

    rows_i = lax.broadcasted_iota(jnp.int32, (Q, Q), 0)
    cols_i = lax.broadcasted_iota(jnp.int32, (Q, Q), 1)
    tri = jnp.where(rows_i >= cols_i, 1.0, 0.0).astype(BF16)
    eye = jnp.where(rows_i == cols_i, 1.0, 0.0).astype(BF16)
    ldp[...] = jnp.zeros_like(ldp)
    for i in range(3):
        ldp[i * STRIDE : i * STRIDE + heads, :] = ld[...]
    lane = lax.broadcasted_iota(jnp.int32, (1, LANES), 1)
    er = lax.broadcasted_iota(jnp.int32, (LANES, width), 0)
    ec = lax.broadcasted_iota(jnp.int32, (LANES, width), 1)
    first = (er % STRIDE) * P_SIZE
    expand[...] = jnp.where(
        (ec >= first) & (ec < first + P_SIZE) & (er < 3 * STRIDE), 1.0, 0.0
    ).astype(BF16)

    def packed(value):
        high, middle, low = split3(value)
        rest = jnp.where(lane < 2 * STRIDE, middle.astype(F32), low.astype(F32))
        return jnp.where(lane < STRIDE, high.astype(F32), rest).astype(BF16)

    hp = runrow.shape[1]
    for b in range(count):
        blk = slice(b * Q, (b + 1) * Q)
        flags = jnp.broadcast_to(st[0:1, blk].astype(F32), (LANES, Q)).astype(BF16)
        seg_col = nt(tri, flags)
        seg_row = nt(flags[0:16], tri)
        parts = split3(ldp[:, blk])
        run = nt(tri, parts[0]) + (nt(tri, parts[1]) + nt(tri, parts[2]))
        run_r = nt(parts[0][0:hp], tri) + (nt(parts[1][0:hp], tri) + nt(parts[2][0:hp], tri))
        decay = nt(eye, parts[0]) + nt(eye, parts[1]) + nt(eye, parts[2])
        gain2 = minus_expm1(2.0 * decay)
        gain = jnp.sqrt(gain2)
        runrow[b] = run_r * LOG2E
        colterm[b] = run * LOG2E - (0.5 * LOG2E) * jnp.log(gain2)
        last, seg_last = run[Q - 1 : Q], seg_col[Q - 1 : Q]
        tail = jnp.where(seg_col == seg_last, jnp.exp(last - run), 0.0) * gain
        enter = jnp.where(seg_col == 0.0, jnp.exp(run), 0.0)
        through = jnp.broadcast_to(jnp.where(seg_last == 0.0, jnp.exp(last), 0.0), (16, LANES))
        factor[b, 0] = packed(tail)
        factor[b, 1] = packed(enter)
        passing[b] = nn(packed(through), expand[...])[0:8]
        keep = (cols_i >= rows_i) & (
            jnp.broadcast_to(seg_row[0:1], (Q, Q)) == jnp.broadcast_to(seg_col[:, 0:1], (Q, Q))
        )
        bias[b] = jnp.where(keep, 0.0, -1e30)
        keys_t[b] = nt(eye[0:N, 0:N], bm[blk, :]).astype(BF16)
        reads_t[b] = nt(eye[0:N, 0:N], cm[blk, :]).astype(BF16)
        scores[b] = nt(bm[blk, :], cm[blk, :])

    pl.semaphore_wait(barrier, bits + hd - 1)
    for copy in loads:
        copy.wait()

    F, T, T1 = slice(0, N), slice(N, N + 8), slice(N, N + 1)
    B, TB = slice(N + 8, 2 * N + 8), slice(2 * N + 8, 2 * N + 16)
    portion = N + 8

    def states(w):
        wide = slice(w * WIDE, (w + 1) * WIDE)
        ex = expand[:, wide]
        for b in range(count):
            blk = slice(b * Q, (b + 1) * Q)
            tx = nn(factor[b, 0], ex)
            tail_x[blk, wide] = tx
            hi, lo = split2(xs[blk, wide].astype(F32) * tx)
            t_hi[blk, wide] = hi
            t_lo[blk, wide] = lo
            own = nn(keys_t[b], hi) + nn(keys_t[b], lo)
            local_s[b, 2 * w] = own[:, :LANES]
            local_s[b, 2 * w + 1] = own[:, LANES:]
            hi, lo = split2(dy[blk, wide].astype(F32) * nn(factor[b, 1], ex))
            e_hi[blk, wide] = hi
            e_lo[blk, wide] = lo
            own = nn(reads_t[b], hi) + nn(reads_t[b], lo)
            local_a[b, 2 * w] = own[:, :LANES]
            local_a[b, 2 * w + 1] = own[:, LANES:]
        for k in (2 * w, 2 * w + 1):
            col = slice(k * LANES, (k + 1) * LANES)
            forward, backward, through = local_s[0, k], local_a[count - 1, k], passing[0, :, col]
            for b in range(1, count):
                forward = local_s[b, k] + passing[b, 0:1, col] * forward
                through = through * passing[b, :, col]
            for b in range(count - 2, -1, -1):
                backward = local_a[b, k] + passing[b, 0:1, col] * backward
            agg[k, F] = forward
            agg[k, T] = through
            agg[k, B] = backward
            agg[k, TB] = through

    def owned(core, k):
        return core * half + (k + (half - 1) * (1 - core)) % half

    stage0 = [remote(agg.at[owned(1 - core, k)], got0.at[k], 0, k, 0) for k in range(half)]

    I, O = slice(0, N), slice(N, 2 * N)
    forwarded = 2
    copies = {}
    ahead = {}

    def merge(target, mine, theirs, upper):
        def low(s):
            return jnp.where(upper, theirs(s), mine(s))

        def high(s):
            return jnp.where(upper, mine(s), theirs(s))

        target[F] = high(F) + high(T1) * low(F)
        target[B] = low(B) + low(T1) * high(B)
        through = low(T) * high(T)
        target[T] = through
        target[TB] = through

    near, far = bits - 2, bits - 1
    lo_bit, hi_bit = bit[near], bit[far]
    inner = lo_bit + hi_bit == 1
    outer = lo_bit + hi_bit != 1
    started = []

    def begin(copy, condition=None):
        started.append((copy, condition))
        guarded(copy.start, condition)
        return copy

    def guarded(action, condition):
        if condition is None:
            action()
        else:
            pl.when(condition)(action)

    def chip_send(d, k):
        if d < near:
            copies[d, k] = begin(remote(chip.at[d - 1, k], got.at[d - 1, k], d, k, d))
            return
        source = chip.at[d - 1, k]
        copies["near", k] = begin(remote(
            source.at[pl.ds(pl.multiple_of(lo_bit * portion, 8), portion)],
            got.at[d - 1, k, pl.ds(0, portion)], near, k, near,
        ))
        if k >= forwarded:
            copies["more", k] = begin(remote(
                source.at[pl.ds(pl.multiple_of((1 - lo_bit) * portion, 8), N)],
                more.at[k], bits + 1, k, near,
            ), inner)

    def stage_core(k):
        stage0[k].wait_recv()
        merge(
            chip.at[0, k], lambda s: agg[owned(core, k), s], lambda s: got0[k, s], core == 1
        )
        inout[k] = jnp.zeros((2 * N, LANES), F32)
        ahead[k] = (jnp.ones((1, LANES), F32), jnp.ones((1, LANES), F32))
        chip_send(1, k)

    def stage_chip(d, k):
        copies[d, k].wait_recv()
        upper = bit[d] == 1
        from_before, from_after = ahead[k]
        theirs, mine = got.at[d - 1, k], chip.at[d - 1, k]
        inout[k, I] = inout[k, I] + jnp.where(upper, from_before, 0.0) * theirs[F]
        inout[k, O] = inout[k, O] + jnp.where(upper, 0.0, from_after) * theirs[B]
        ahead[k] = (
            jnp.where(upper, from_before * theirs[T1], from_before),
            jnp.where(upper, from_after, from_after * theirs[T1]),
        )
        merge(chip.at[d, k], lambda s: mine[s], lambda s: theirs[s], upper)
        chip_send(d + 1, k)

    def stage_near(k):
        copies["near", k].wait_recv()
        theirs, mine = got.at[near - 1, k], chip.at[near - 1, k]
        own = jnp.where(hi_bit == 0, mine[F], mine[B])
        both = own + mine[T1] * theirs[F]
        if k >= forwarded:
            guarded(copies["more", k].wait_recv, outer)
            both = jnp.where(inner, both, more[k] + theirs[T1] * own)
        pair[k] = both
        copies["far", k] = begin(
            remote(pair.at[k], across.at[k], far, k, far), inner if k < forwarded else None
        )

    def stage_forward(k):
        guarded(copies["far", k].wait_recv, outer)
        copies["on", k] = begin(remote(across.at[k], across.at[k], bits + 2, k, near), outer)

    def stage_far(k):
        if k < forwarded:
            guarded(copies["on", k].wait_recv, inner)
        else:
            copies["far", k].wait_recv()
        theirs, beyond = got.at[near - 1, k], across[k]
        near_side = jnp.where(inner, theirs[F], theirs[F] + theirs[T1] * beyond)
        from_before, from_after = ahead[k]
        far_before = jnp.where(hi_bit == 1, beyond, 0.0)
        far_after = jnp.where(hi_bit == 0, beyond, 0.0)
        enter0 = inout[k, I] + from_before * jnp.where(lo_bit == 1, near_side, far_before)
        leave1 = inout[k, O] + from_after * jnp.where(lo_bit == 0, near_side, far_after)
        own = agg.at[owned(core, k)]
        odd = core == 1
        low_f = jnp.where(odd, got0[k, F], own[F])
        low_t = jnp.where(odd, got0[k, T1], own[T1])
        high_b = jnp.where(odd, own[B], got0[k, B])
        high_t = jnp.where(odd, own[T1], got0[k, T1])
        enter1 = low_f + low_t * enter0
        leave0 = high_b + high_t * leave1
        final[owned(core, k), I] = jnp.where(odd, enter1, enter0)
        final[owned(core, k), O] = jnp.where(odd, leave1, leave0)
        other[k, I] = jnp.where(odd, enter0, enter1)
        other[k, O] = jnp.where(odd, leave0, leave1)
        copies["core", k] = begin(remote(other.at[k], final.at[owned(core, k)], bits, k, 0))

    mixed[...] = jnp.zeros_like(mixed)
    head_mask = [
        jnp.where(lane < P_SIZE, 1.0, 0.0).astype(BF16),
        jnp.where(lane < P_SIZE, 0.0, 1.0).astype(BF16),
    ]
    sub = Q // 2

    def intra(k):
        col = slice(k * LANES, (k + 1) * LANES)
        for b in range(count):
            for part_s in range(2):
                t0 = part_s * sub
                s_in = slice(part_s * sub, (part_s + 1) * sub)
                s_at = slice(b * Q + part_s * sub, b * Q + (part_s + 1) * sub)
                t_at = slice(b * Q + t0, (b + 1) * Q)
                x, u = xs[s_at, col], dy[t_at, col]
                total, mix = None, None
                for h in range(2):
                    head = 2 * k + h
                    uh = u * head_mask[h]
                    pairing = nt(x, uh)
                    within = jnp.exp2(
                        (runrow[b, head : head + 1, t0:] - colterm[b, s_in, head : head + 1])
                        + bias[b, s_in, t0:]
                    )
                    hi, lo = split2(within * scores[b, s_in, t0:])
                    product = nn(hi, uh) + nn(lo, uh)
                    total = product if total is None else total + product
                    mix = within * pairing if mix is None else mix + within * pairing
                mixed[b, s_in, t0:] += mix
                group[s_at, col] = total

    wides = width // WIDE
    middle = wides // 2
    states(middle)
    stage0[0].start()
    for w in range(middle):
        states(w)
        states(middle + 1 + w)
        for k in (2 * w + 1, 2 * w + 2):
            stage0[k].start()
        for k in range(max(0, 2 * w - 1), 2 * w + 1):
            stage_core(k)
    intra(0)
    for k in range(half - 2, half):
        stage_core(k)
    for k in range(1, tiles):
        intra(k)
        if near == 1 and k in (4, 7):
            stage_near(0 if k == 4 else 1)
    for b in range(count):
        blk = slice(b * Q, (b + 1) * Q)
        hi, lo = split2(mixed[b])
        part[0, blk] = nn(hi, cm[blk, :]) + nn(lo, cm[blk, :])
        hi, lo = split2(mixed[b].T)
        part[1, blk] = nn(hi, bm[blk, :]) + nn(lo, bm[blk, :])
    for d in range(1, near):
        for k in range(half):
            stage_chip(d, k)
    if near > 1:
        for k in range(forwarded):
            stage_near(k)
    share = count * Q // hd
    sums[...] = jnp.zeros_like(sums)

    def rs_copy(dest):
        return pltpu.make_async_remote_copy(
            src_ref=part.at[:, pl.ds(dest * share, share)], dst_ref=rs_got.at[row],
            send_sem=rs_send.at[dest], recv_sem=rs_recv.at[row],
            device_id={"head": dest}, device_id_type=MESH,
        )

    def state_of(b, w, forward):
        wide = slice(w * WIDE, (w + 1) * WIDE)
        rows, chain = (I, range(b)) if forward else (O, range(count - 1, b, -1))
        local = local_s if forward else local_a
        value = jnp.concatenate([final[2 * w, rows], final[2 * w + 1, rows]], axis=1)
        for at in chain:
            value = (
                jnp.concatenate([local[at, 2 * w], local[at, 2 * w + 1]], axis=1)
                + passing[at, 0:1, wide] * value
            )
        return jnp.concatenate(split2(value), axis=0)

    def outside(b, w):
        blk, wide = slice(b * Q, (b + 1) * Q), slice(w * WIDE, (w + 1) * WIDE)
        both = state_of(b, w, False)
        stacked[b, w] = both
        sums[b, 0] += nt(t_hi[blk, wide], both)
        part[0, blk] += nt(t_lo[blk, wide], both[0:N])
        both = state_of(b, w, True)
        sums[b, 1] += nt(e_hi[blk, wide], both)
        part[1, blk] += nt(e_lo[blk, wide], both[0:N])

    def gradient(b, w):
        blk, wide = slice(b * Q, (b + 1) * Q), slice(w * WIDE, (w + 1) * WIDE)
        keys2 = jnp.concatenate([bm[blk, :], bm[blk, :]], axis=1)
        state_x = nn(keys2, stacked[b, w])
        gx_out[blk, wide] = (group[blk, wide] + state_x * tail_x[blk, wide]).astype(BF16)

    def finish(w):
        for b in range(count):
            outside(b, w)
            gradient(b, w)

    for k in range(forwarded):
        stage_forward(k)
    stage_near(2)
    for k in range(forwarded):
        stage_far(k)
    stage_near(3)
    stage_far(2)
    copies["core", 0].wait_recv()
    finish(wides // 2)
    stage_near(4)
    stage_far(3)
    for k in (1, 2):
        copies["core", k].wait_recv()
    finish(0)
    finish(wides // 2 + 1)
    stage_far(4)
    for k in (3, 4):
        copies["core", k].wait_recv()
    for b in range(count):
        blk = slice(b * Q, (b + 1) * Q)
        outside(b, 1)
        outside(b, wides - 1)
        part[0, blk] += sums[b, 0, :, :N] + sums[b, 0, :, N:]
        part[1, blk] += sums[b, 1, :, :N] + sums[b, 1, :, N:]
        for dest in range(hd):
            if b * Q < (dest + 1) * share <= (b + 1) * Q:
                @pl.when(row != dest)
                def _(dest=dest):
                    rs_copy(dest).start()
    for b in range(count):
        for w in (1, wides - 1):
            gradient(b, w)
    mine = pl.ds(pl.multiple_of(row * share, share), share)
    gb_out[...] = part[0, mine]
    gc_out[...] = part[1, mine]
    for source in range(hd):
        @pl.when(row != source)
        def _(source=source):
            pltpu.make_async_remote_copy(
                src_ref=part.at[:, pl.ds(0, share)], dst_ref=rs_got.at[source],
                send_sem=rs_send.at[source], recv_sem=rs_recv.at[source],
                device_id={"head": source}, device_id_type=MESH,
            ).wait_recv()
            gb_out[...] += rs_got[source, 0]
            gc_out[...] += rs_got[source, 1]
    for dest in range(hd):
        @pl.when(row != dest)
        def _(dest=dest):
            rs_copy(dest).wait_send()
    for copy in stage0:
        copy.wait_send()
    for copy, condition in started:
        guarded(copy.wait_send, condition)


def shards(ctx, hd, xs, bmat, cmat, logdecay, starts, output_cotangent):
    tokens, width = xs.shape
    heads = logdecay.shape[0]
    count = tokens // Q
    tiles = width // LANES
    half = tiles // 2
    bits = ctx.bit_length() - 1
    head_rows = (heads + 15) // 16 * 16
    share = tokens // hd
    packet = 2 * N + 16
    scratch = [
        pltpu.VMEM((tokens, width), BF16),
        pltpu.VMEM((tokens, width), BF16),
        pltpu.VMEM((count, width // WIDE, 2 * N, WIDE), BF16),
        pltpu.SemaphoreType.DMA((2,)),
        pltpu.VMEM((half, N, LANES), F32),
        pltpu.VMEM((half, N, LANES), F32),
        pltpu.VMEM((half, N, LANES), F32),
        pltpu.VMEM((count, 2, Q, WIDE), F32),
        pltpu.VMEM((LANES, tokens), F32),
        pltpu.VMEM((count, Q, LANES), F32),
        pltpu.VMEM((count, head_rows, Q), F32),
        pltpu.VMEM((count, 2, Q, LANES), BF16),
        pltpu.VMEM((LANES, width), BF16),
        pltpu.VMEM((count, 8, width), F32),
        pltpu.VMEM((count, Q, Q), F32),
        pltpu.VMEM((count, Q, Q), F32),
        pltpu.VMEM((count, Q, Q), F32),
        pltpu.VMEM((count, N, Q), BF16),
        pltpu.VMEM((count, N, Q), BF16),
        pltpu.VMEM((tokens, width), F32),
        pltpu.VMEM((tokens, width), BF16),
        pltpu.VMEM((tokens, width), BF16),
        pltpu.VMEM((tokens, width), BF16),
        pltpu.VMEM((tokens, width), BF16),
        pltpu.VMEM((tokens, width), F32),
        pltpu.VMEM((count, tiles, N, LANES), F32),
        pltpu.VMEM((count, tiles, N, LANES), F32),
        pltpu.VMEM((tiles, packet, LANES), F32),
        pltpu.VMEM((half, packet, LANES), F32),
        pltpu.VMEM((bits - 1, half, packet, LANES), F32),
        pltpu.VMEM((bits - 1, half, packet, LANES), F32),
        pltpu.VMEM((half, 2 * N, LANES), F32),
        pltpu.VMEM((half, 2 * N, LANES), F32),
        pltpu.VMEM((tiles, 2 * N, LANES), F32),
        pltpu.VMEM((2, tokens, N), F32),
        pltpu.VMEM((hd, 2, share, N), F32),
        pltpu.SemaphoreType.DMA((bits + 3, half)),
        pltpu.SemaphoreType.DMA((bits + 3, half)),
        pltpu.SemaphoreType.DMA((hd,)),
        pltpu.SemaphoreType.DMA((hd,)),
    ]
    vmem = pl.BlockSpec(memory_space=pltpu.VMEM)
    anywhere = pl.BlockSpec(memory_space=pl.ANY)
    results = pl.pallas_call(
        functools.partial(kernel, ctx, hd, heads, count),
        out_shape=(
            pltpu.VMEM((tokens, width), BF16),
            pltpu.VMEM((share, N), F32),
            pltpu.VMEM((share, N), F32),
        ),
        in_specs=[anywhere, vmem, vmem, vmem, vmem, anywhere],
        out_specs=(vmem, vmem, vmem),
        scratch_shapes=scratch,
        compiler_params=pltpu.CompilerParams(
            collective_id=0, has_side_effects=True, vmem_limit_bytes=56 * 1024 * 1024
        ),
    )(xs, bmat, cmat, logdecay, starts.reshape(1, tokens), output_cotangent)
    return results


def solution(mesh):
    in_specs = (
        P("ctx", "head"),
        P("ctx", None),
        P("ctx", None),
        P("head", "ctx"),
        P("ctx"),
        P("ctx", "head"),
    )
    out_specs = (P("ctx", "head"), P(("ctx", "head"), None), P(("ctx", "head"), None))
    body = functools.partial(shards, mesh.shape["ctx"], mesh.shape["head"])
    return jax.shard_map(body, mesh=mesh, in_specs=in_specs, out_specs=out_specs, check_vma=False)
```
